32 devices in a mesh: groups: 2 (over y), expert: 8 (over z, x), dp: 2 (over core).
Axes of the slice: x: 2, y: 2, z: 4, core: 2. Of those that a mesh axis runs over, the one named last changes fastest.
Arguments:
- grad_out: bfloat16 [4096, 2048], P(('groups', 'expert', 'dp')), parts along dimension 0, may hold values from -3 to 3
- pre_act: bfloat16 [4096, 2, 2, 512], P(('groups', 'expert', 'dp')), parts along dimension 0, may hold values from -6 to 6
- routes: int32 [4096, 2], P(('groups', 'expert', 'dp')), parts along dimension 0, may hold values from 0 to 7, all different within a row; in each aligned block of 128 rows (0 to 127, 128 to 255, ...) at most 128 rows name the same one
- gate_prob: float32 [4096, 2], P(('groups', 'expert', 'dp')), parts along dimension 0, may hold values from 0.1 to 1
- down_weight: bfloat16 [8, 512, 2048], P('expert', 'dp'), may hold values from -0.25 to 0.25
Outputs:
- d_pre: bfloat16 [4096, 2, 2, 512], P(('groups', 'expert', 'dp')), parts along dimension 0
- grad_down: bfloat16 [16, 512, 2048], P(('groups', 'expert'), 'dp'), parts along dimension 0
The draws below stay inside these ranges and needn't reach their ends.
There are 2 independent parts, one for each index of `groups`. The reference program is written for one: setup_inputs(seed, part) draws one part's arguments, and reference() takes and returns one part's arrays. A program takes and returns all parts, laid end to end along the dimension named above; an argument that names none is the same for every part. Nothing has to cross between parts.
Inputs may be any that keep to these rules, and one draw needn't show every extreme that they name: Each token names 2 different experts. Within the 128 tokens of one device, each expert is named by at most 128 routes, a bound that some block reaches.
All inputs are finite; a program needn't handle non-finite values.
Results may differ from the reference program's by a relative error of at most 0.0065.
Values may be sent and summed in bfloat16 or wider, within the bound.
A program may use at most 64 MiB of HBM per device.

```python
import math
import jax
import jax.numpy as jnp
import numpy as np
from jax import lax

D = 2048
F = 512
TOPK = 2
TOK_DEV = 128
EXPERTS = 8
TOKENS = 2048
CAP = 128
N_EXPERT = 8
N_DP = 2


def shard_levels(own_key, dims, pieces, smallest, top_value):
    loudness, own = 1.0, jax.random.fold_in(own_key, 6)
    for axis_at, parts in pieces:
        draws = jnp.exp(jax.random.uniform(jax.random.fold_in(own, axis_at), (parts,), jnp.float32, smallest / len(pieces), top_value / len(pieces)))
        loudness = loudness * jnp.repeat(draws, dims[axis_at] // parts).reshape([-1 if axis == axis_at else 1 for axis in range(len(dims))])
    return loudness


def routed_block(stream_key, own, number, rows, number_of, top, limit, skew):
    sequence = jax.random.permutation(stream_key, number_of)
    crowded, usual = portions_of(number_of, rows * top, limit, skew, True), portions_of(number_of, rows * top, limit, skew, False)
    places = jnp.arange(number_of)

    def named(sizes, offset_by):
        used = int((sizes > 0).sum())
        fixed = max(1, used // 4)
        shifted = fixed + (places - fixed + offset_by * (used - fixed)) % max(1, number_of - fixed)
        return jnp.zeros((number_of,), jnp.int32).at[sequence[jnp.where(places < fixed, places, shifted)]].set(jnp.asarray(sizes, jnp.int32))

    sizes = jnp.where(number % 4 == 0, named(crowded, number // 4), named(usual, number - number // 4 - 1))
    mixed = jax.random.permutation(jax.random.fold_in(own, 3), number_of)
    source_of, sink = mixed[0:number_of // 2 * 2:2], mixed[1:number_of // 2 * 2:2]
    slack = jnp.minimum(sizes[source_of] - 1, limit - sizes[sink]) // 2
    slack = jnp.where((source_of == sequence[0]) | (sink == sequence[0]) | (sizes[sink] == 0), 0, jnp.maximum(slack, 0))
    shifted = jax.random.randint(jax.random.fold_in(own, 4), (number_of // 2,), 0, 1 << 20) % (slack + 1)
    sizes = sizes.at[source_of].add(-shifted).at[sink].add(shifted)
    items = jnp.searchsorted(jnp.cumsum(sizes), jnp.arange(rows * top), side="right").astype(jnp.int32)
    listing = items.reshape(top, rows).T
    listing = listing[jax.random.permutation(jax.random.fold_in(own, 1), rows)]
    offset_by = jax.random.randint(jax.random.fold_in(own, 2), (rows, 1), 0, top)
    return jnp.take_along_axis(listing, (jnp.arange(top)[None, :] + offset_by) % top, axis=1)


def portions_of(amount, total, bound, skew, full):
    loads = [(1 << 20) // math.isqrt(rank ** skew) + 1 for rank in range(1, amount + 1)]
    largest = bound if full else min(bound, max(-(-total // amount), total * loads[0] // sum(loads)))
    least = 1 if total - largest >= amount - 1 else 0
    holding, surplus = [largest] + [least] * (amount - 1), total - largest - least * (amount - 1)
    while surplus > 0:
        movable = [i for i in range(1, amount) if holding[i] < largest] or [i for i in range(1, amount) if holding[i] < bound]
        whole, remaining = sum([loads[i] for i in movable]), surplus
        for i in movable:
            more = min(bound - holding[i], max(1, remaining * loads[i] // whole), surplus)
            holding[i] = holding[i] + more
            surplus = surplus - more
    return np.array(holding)


def bell_draw(own_key, shape, deviation, most, split=(), kind=jnp.bfloat16):
    entries = deviation * jax.random.normal(own_key, shape, jnp.float32)
    if split:
        entries = entries * shard_levels(own_key, shape, split, -0.22, 0.18)
    return jnp.clip(entries, -most, most).astype(kind)


def setup_inputs(seed: int = 0, part: int = 0) -> dict:
    arg_keys = jax.random.split(jax.random.key(seed), 6)
    part_splits = jax.random.split(jax.random.fold_in(arg_keys[5], part), 6)
    grad_out = bell_draw(part_splits[0], (TOKENS, D), 0.5, 3.0, ((0, 16),))
    pre_act = bell_draw(part_splits[1], (TOKENS, TOPK, 2, F), 1.0, 6.0, ((0, 16),))
    routes_keys = jax.random.split(jax.random.fold_in(part_splits[2], 1), TOKENS // TOK_DEV)
    routes_turns = jax.random.permutation(jax.random.fold_in(part_splits[2], 3), TOKENS // TOK_DEV)
    routes = jax.vmap(lambda own, number: routed_block(jax.random.fold_in(part_splits[2], 2), own, number, TOK_DEV, EXPERTS, TOPK, CAP, 1))(routes_keys, routes_turns).reshape((TOKENS, TOPK))
    gate_prob = jnp.clip(0.1 + 0.9 * jax.random.uniform(part_splits[3], (TOKENS, TOPK), jnp.float32) ** shard_levels(part_splits[3], (TOKENS, TOPK), ((0, 16),), -0.2, 0.2), 0.1, 1.0)
    down_weight = bell_draw(arg_keys[4], (EXPERTS, F, D), F ** -0.5, 0.25, ((0, 8), (1, 2)))
    return {"grad_out": grad_out, "pre_act": pre_act, "routes": routes, "gate_prob": gate_prob, "down_weight": down_weight}


def gate_hidden(gate_pre, up_pre):
    sigmoid_gate = jax.nn.sigmoid(gate_pre)
    return (gate_pre * sigmoid_gate * up_pre).astype(jnp.bfloat16)


def activation_grads(hidden_grad, gate_pre, up_pre):
    sigmoid_gate = jax.nn.sigmoid(gate_pre)
    upstream = hidden_grad.astype(jnp.float32)
    gate_part = upstream * up_pre * sigmoid_gate * (1.0 + gate_pre * (1.0 - sigmoid_gate))
    up_part = upstream * (gate_pre * sigmoid_gate)
    return jnp.concatenate([gate_part, up_part], axis=-1).astype(jnp.bfloat16)


def reference(grad_out, pre_act, routes, gate_prob, down_weight):
    route_count = TOKENS * TOPK
    scaled = (gate_prob[:, :, None] * grad_out[:, None, :].astype(jnp.float32)).astype(jnp.bfloat16).reshape(route_count, D)
    pre_rows = pre_act.astype(jnp.float32).reshape(route_count, 2 * F)
    gate_pre = pre_rows[:, :F]
    up_pre = pre_rows[:, F:]
    hidden = gate_hidden(gate_pre, up_pre)
    token_index = jnp.arange(TOKENS, dtype=jnp.int32)
    half_of = (token_index // TOK_DEV) % N_DP
    group_key = (routes * N_DP + half_of[:, None]).reshape(route_count).astype(jnp.int32)
    sorted_index = jnp.argsort(group_key, stable=True).astype(jnp.int32)
    group_size = jnp.bincount(group_key, length=EXPERTS * N_DP).astype(jnp.int32)
    group_start = (jnp.cumsum(group_size) - group_size).astype(jnp.int32)
    window_rows = N_EXPERT * CAP
    sorted_scaled = jnp.concatenate([scaled[sorted_index], jnp.zeros((window_rows, D), jnp.bfloat16)], axis=0)
    sorted_hidden = jnp.concatenate([hidden[sorted_index], jnp.zeros((window_rows, F), jnp.bfloat16)], axis=0)
    position = jnp.arange(window_rows, dtype=jnp.int32)

    def per_expert(expert_id):
        weight_rows = down_weight[expert_id]
        summed = jnp.zeros((F, D), jnp.float32)
        grad_list = []
        for half_index in range(N_DP):
            group = expert_id * N_DP + half_index
            first_row = group_start[group]
            row_total = group_size[group]
            scaled_block = lax.dynamic_slice_in_dim(sorted_scaled, first_row, window_rows, 0)
            hidden_block = lax.dynamic_slice_in_dim(sorted_hidden, first_row, window_rows, 0)
            occupied = (position < row_total)[:, None]
            scaled_block = jnp.where(occupied, scaled_block, jnp.zeros_like(scaled_block))
            hidden_block = jnp.where(occupied, hidden_block, jnp.zeros_like(hidden_block))
            partial_value = lax.dot_general(hidden_block, scaled_block, (((0,), (0,)), ((), ())), preferred_element_type=jnp.float32)
            rounded = lax.optimization_barrier(partial_value.astype(jnp.bfloat16))
            summed = summed + rounded.astype(jnp.float32)
            block_grad = lax.dot_general(scaled_block, weight_rows, (((1,), (1,)), ((), ())), preferred_element_type=jnp.float32)
            grad_list.append(block_grad.astype(jnp.bfloat16))
        return summed.astype(jnp.bfloat16), jnp.stack(grad_list)

    grad_down, grad_blocks = lax.map(per_expert, jnp.arange(EXPERTS, dtype=jnp.int32))
    sorted_key = group_key[sorted_index]
    rank_in_group = jnp.arange(route_count, dtype=jnp.int32) - group_start[sorted_key]
    flat_index = (sorted_key * window_rows + rank_in_group).astype(jnp.int32)
    grad_sorted = grad_blocks.reshape(EXPERTS * N_DP * window_rows, F)[flat_index]
    hidden_grad = jnp.zeros((route_count, F), jnp.bfloat16).at[sorted_index].set(grad_sorted)
    d_pre = activation_grads(hidden_grad, gate_pre, up_pre).reshape(TOKENS, TOPK, 2, F)
    return d_pre, grad_down
```

```python
import jax
import jax.numpy as jnp
from jax import lax
from jax.sharding import PartitionSpec as P


def gate_hidden(gate_pre, up_pre):
    sigmoid_gate = jax.nn.sigmoid(gate_pre)
    return (gate_pre * sigmoid_gate * up_pre).astype(jnp.bfloat16)


def activation_grads(hidden_grad, gate_pre, up_pre):
    sigmoid_gate = jax.nn.sigmoid(gate_pre)
    upstream = hidden_grad.astype(jnp.float32)
    gate_part = upstream * up_pre * sigmoid_gate * (1.0 + gate_pre * (1.0 - sigmoid_gate))
    up_part = upstream * (gate_pre * sigmoid_gate)
    return jnp.concatenate([gate_part, up_part], axis=-1).astype(jnp.bfloat16)


def pack_rows(row_values, slot_index, peer_count, capacity):
    row_width = row_values.shape[1]
    buffer = (
        jnp.zeros((peer_count * capacity, row_width), row_values.dtype)
        .at[slot_index]
        .set(row_values)
    )
    return buffer.reshape(peer_count, capacity, row_width)


def expert_work(scaled_rows, hidden_rows, full_weight):
    dims_back = (((1,), (1,)), ((), ()))
    dims_outer = (((0,), (0,)), ((), ()))
    hidden_grad = lax.dot_general(
        scaled_rows, full_weight, dims_back, preferred_element_type=jnp.float32
    ).astype(jnp.bfloat16)
    partial_value = lax.dot_general(
        hidden_rows, scaled_rows, dims_outer, preferred_element_type=jnp.float32
    )
    return (hidden_grad, partial_value)


def balanced_work(got_scaled, got_hidden, full_weight):
    peer_count = got_scaled.shape[0]
    capacity = got_scaled.shape[1]
    slots_all = peer_count * capacity
    scaled_rows = got_scaled.reshape(slots_all, got_scaled.shape[2])
    hidden_rows = got_hidden.reshape(slots_all, got_hidden.shape[2])
    hidden_grad, partial_value = expert_work(scaled_rows, hidden_rows, full_weight)
    return (hidden_grad.reshape(peer_count, capacity, hidden_grad.shape[1]), partial_value)


def packed_shards(grad_out, pre_act, routes, gate_prob, down_weight):
    peer_count = lax.axis_size("expert")
    token_rows = routes.shape[0]
    route_width = routes.shape[1]
    route_count = token_rows * route_width
    capacity = 4 * route_count // peer_count
    feature_count = grad_out.shape[1]
    hidden_count = pre_act.shape[3]
    scaled = (
        (gate_prob[:, :, None] * grad_out[:, None, :].astype(jnp.float32))
        .astype(jnp.bfloat16)
        .reshape(route_count, feature_count)
    )
    pre_rows = pre_act.reshape(route_count, 2 * hidden_count)
    expert_ids = routes.reshape(route_count)
    one_hot = (expert_ids[:, None] == jnp.arange(peer_count, dtype=jnp.int32)[None, :]).astype(
        jnp.int32
    )
    slot_rank = jnp.sum(jnp.cumsum(one_hot, axis=0) * one_hot, axis=1) - 1
    sent_counts = jnp.sum(one_hot, axis=0).reshape(peer_count, 1)
    slot_index = expert_ids * capacity + slot_rank
    full_weight = lax.all_gather(down_weight[0], "dp", axis=0, tiled=True)
    got_scaled, got_pre, arrived = (
        lax.all_to_all(
            pack_rows(scaled, slot_index, peer_count, capacity),
            "expert",
            split_axis=0,
            concat_axis=0,
            tiled=True,
        ),
        lax.all_to_all(
            pack_rows(pre_rows, slot_index, peer_count, capacity),
            "expert",
            split_axis=0,
            concat_axis=0,
            tiled=True,
        ),
        lax.all_to_all(sent_counts, "expert", split_axis=0, concat_axis=0, tiled=True),
    )
    pre_float = got_pre.astype(jnp.float32)
    gate_pre = pre_float[:, :, :hidden_count]
    up_pre = pre_float[:, :, hidden_count:]
    got_hidden = gate_hidden(gate_pre, up_pre)
    hidden_grad, partial_value = balanced_work(got_scaled, got_hidden, full_weight)
    slot_grads = activation_grads(hidden_grad, gate_pre, up_pre)
    returned = lax.all_to_all(slot_grads, "expert", split_axis=0, concat_axis=0, tiled=True)
    d_pre = returned.reshape(peer_count * capacity, 2 * hidden_count)[slot_index]
    summed = lax.psum_scatter(
        partial_value.astype(jnp.bfloat16), "dp", scatter_dimension=0, tiled=True
    )
    return (d_pre.reshape(token_rows, route_width, 2, hidden_count), summed[None])


def dense_shards(grad_out, pre_act, routes, gate_prob, down_weight):
    peer_count = lax.axis_size("expert")
    me = lax.axis_index("expert")
    token_rows, feature_count = grad_out.shape
    hidden_count = pre_act.shape[3]
    pre_float = pre_act.astype(jnp.float32)
    gate_pre, up_pre = pre_float[:, :, 0, :], pre_float[:, :, 1, :]
    hidden = gate_hidden(gate_pre, up_pre).reshape(token_rows, 2 * hidden_count)
    all_routes = lax.all_gather(routes, "expert", axis=0, tiled=True)
    all_prob = lax.all_gather(gate_prob, "expert", axis=0, tiled=True)
    all_grad = lax.all_gather(grad_out, "expert", axis=0, tiled=True)
    all_hidden = lax.all_gather(hidden, "expert", axis=0, tiled=True)
    full_weight = lax.all_gather(down_weight[0], "dp", axis=0, tiled=True)
    mine = all_routes == me
    factor = jnp.sum(jnp.where(mine, all_prob, 0.0), axis=1, keepdims=True)
    scaled_rows = (factor * all_grad.astype(jnp.float32)).astype(jnp.bfloat16)
    hidden_rows = jnp.where(
        mine[:, :1],
        all_hidden[:, :hidden_count],
        jnp.where(mine[:, 1:], all_hidden[:, hidden_count:], jnp.zeros((), jnp.bfloat16)),
    )
    hidden_grad, partial_value = expert_work(scaled_rows, hidden_rows, full_weight)
    returned = lax.all_to_all(
        hidden_grad.reshape(peer_count, token_rows, hidden_count),
        "expert",
        split_axis=0,
        concat_axis=0,
        tiled=True,
    )
    summed = lax.psum_scatter(
        partial_value.astype(jnp.bfloat16), "dp", scatter_dimension=0, tiled=True
    )
    picked = jnp.zeros((token_rows, 2, hidden_count), jnp.bfloat16)
    for expert in range(peer_count):
        picked = jnp.where(
            (routes == expert)[:, :, None], returned[expert][:, None, :], picked
        )
    d_pre = activation_grads(picked, gate_pre, up_pre)
    return (d_pre.reshape(token_rows, 2, 2, hidden_count), summed[None])


def shards(grad_out, pre_act, routes, gate_prob, down_weight):
    capacity = 4 * routes.shape[0] * routes.shape[1] // lax.axis_size("expert")
    plan = dense_shards if capacity >= routes.shape[0] else packed_shards
    return plan(grad_out, pre_act, routes, gate_prob, down_weight)


def solution(mesh):
    placed = (
        P(("groups", "expert", "dp"), None),
        P(("groups", "expert", "dp"), None, None, None),
        P(("groups", "expert", "dp"), None),
        P(("groups", "expert", "dp"), None),
        P("expert", "dp", None),
    )
    return jax.shard_map(
        shards,
        mesh=mesh,
        in_specs=placed,
        out_specs=(
            P(("groups", "expert", "dp"), None, None, None),
            P(("groups", "expert"), "dp", None),
        ),
        check_vma=False,
    )
```

```python
import functools

import jax
import jax.numpy as jnp
from jax import lax
from jax.experimental import pallas as pl
from jax.experimental.pallas import tpu as pltpu
from jax.sharding import PartitionSpec as P


def gate_hidden(gate_pre, up_pre):
    sigmoid_gate = jax.nn.sigmoid(gate_pre)
    return (gate_pre * sigmoid_gate * up_pre).astype(jnp.bfloat16)


def activation_grads(hidden_grad, gate_pre, up_pre):
    sigmoid_gate = jax.nn.sigmoid(gate_pre)
    upstream = hidden_grad.astype(jnp.float32)
    gate_part = upstream * up_pre * sigmoid_gate * (1.0 + gate_pre * (1.0 - sigmoid_gate))
    up_part = upstream * (gate_pre * sigmoid_gate)
    return jnp.concatenate([gate_part, up_part], axis=-1).astype(jnp.bfloat16)


def pack_rows(row_values, slot_index, peer_count, capacity):
    row_width = row_values.shape[1]
    buffer = (
        jnp.zeros((peer_count * capacity, row_width), row_values.dtype)
        .at[slot_index]
        .set(row_values)
    )
    return buffer.reshape(peer_count, capacity, row_width)


def expert_work(scaled_rows, hidden_rows, full_weight):
    dims_back = (((1,), (1,)), ((), ()))
    dims_outer = (((0,), (0,)), ((), ()))
    hidden_grad = lax.dot_general(
        scaled_rows, full_weight, dims_back, preferred_element_type=jnp.float32
    ).astype(jnp.bfloat16)
    partial_value = lax.dot_general(
        hidden_rows, scaled_rows, dims_outer, preferred_element_type=jnp.float32
    )
    return (hidden_grad, partial_value)


def balanced_work(got_scaled, got_hidden, full_weight):
    peer_count = got_scaled.shape[0]
    capacity = got_scaled.shape[1]
    slots_all = peer_count * capacity
    scaled_rows = got_scaled.reshape(slots_all, got_scaled.shape[2])
    hidden_rows = got_hidden.reshape(slots_all, got_hidden.shape[2])
    hidden_grad, partial_value = expert_work(scaled_rows, hidden_rows, full_weight)
    return (hidden_grad.reshape(peer_count, capacity, hidden_grad.shape[1]), partial_value)


def packed_shards(grad_out, pre_act, routes, gate_prob, down_weight):
    peer_count = lax.axis_size("expert")
    token_rows = routes.shape[0]
    route_width = routes.shape[1]
    route_count = token_rows * route_width
    capacity = 4 * route_count // peer_count
    feature_count = grad_out.shape[1]
    hidden_count = pre_act.shape[3]
    scaled = (
        (gate_prob[:, :, None] * grad_out[:, None, :].astype(jnp.float32))
        .astype(jnp.bfloat16)
        .reshape(route_count, feature_count)
    )
    pre_rows = pre_act.reshape(route_count, 2 * hidden_count)
    expert_ids = routes.reshape(route_count)
    one_hot = (expert_ids[:, None] == jnp.arange(peer_count, dtype=jnp.int32)[None, :]).astype(
        jnp.int32
    )
    slot_rank = jnp.sum(jnp.cumsum(one_hot, axis=0) * one_hot, axis=1) - 1
    sent_counts = jnp.sum(one_hot, axis=0).reshape(peer_count, 1)
    slot_index = expert_ids * capacity + slot_rank
    full_weight = lax.all_gather(down_weight[0], "dp", axis=0, tiled=True)
    got_scaled, got_pre, arrived = (
        lax.all_to_all(
            pack_rows(scaled, slot_index, peer_count, capacity),
            "expert",
            split_axis=0,
            concat_axis=0,
            tiled=True,
        ),
        lax.all_to_all(
            pack_rows(pre_rows, slot_index, peer_count, capacity),
            "expert",
            split_axis=0,
            concat_axis=0,
            tiled=True,
        ),
        lax.all_to_all(sent_counts, "expert", split_axis=0, concat_axis=0, tiled=True),
    )
    pre_float = got_pre.astype(jnp.float32)
    gate_pre = pre_float[:, :, :hidden_count]
    up_pre = pre_float[:, :, hidden_count:]
    got_hidden = gate_hidden(gate_pre, up_pre)
    hidden_grad, partial_value = balanced_work(got_scaled, got_hidden, full_weight)
    slot_grads = activation_grads(hidden_grad, gate_pre, up_pre)
    returned = lax.all_to_all(slot_grads, "expert", split_axis=0, concat_axis=0, tiled=True)
    d_pre = returned.reshape(peer_count * capacity, 2 * hidden_count)[slot_index]
    summed = lax.psum_scatter(
        partial_value.astype(jnp.bfloat16), "dp", scatter_dimension=0, tiled=True
    )
    return (d_pre.reshape(token_rows, route_width, 2, hidden_count), summed[None])


CHUNKS = 2
TILE = 512
MESH = pl.DeviceIdType.MESH


def source_at(z, turn, planes):
    reach = jnp.minimum(z, planes - 1 - z)
    step = (turn + 1) // 2
    near = jnp.where(turn % 2 == 1, z - step, z + step)
    far = jnp.where(2 * z <= planes - 1, turn, planes - 1 - turn)
    return jnp.where(turn <= 2 * reach, near, far)


def dense_kernel(
    peers,
    grad_ref,
    pre_ref,
    meta_ref,
    weight_ref,
    d_pre_ref,
    down_ref,
    tokens,
    hiddens,
    cross_out,
    cross_in,
    metas,
    columns,
    weight,
    chosen,
    back_sum,
    back_out,
    back_in,
    total,
    half_out,
    half_in,
    zg_send,
    zg_recv,
    zh_send,
    zh_recv,
    xg_send,
    xg_recv,
    xh_send,
    xh_recv,
    back_send,
    back_recv,
    meta_send,
    meta_recv,
    dp_send,
    dp_recv,
):
    planes = peers // 2
    me = lax.axis_index("expert")
    core = lax.axis_index("dp")
    z, x = me // 2, me % 2
    across = z * 2 + 1 - x
    rows, width = grad_ref.shape
    units = weight.shape[0]
    half = units // 2
    part = rows // CHUNKS
    low = pl.multiple_of(core * half, half)
    other = pl.multiple_of((1 - core) * half, half)

    def remote(src, dst, send, recv, where):
        return pltpu.make_async_remote_copy(
            src_ref=src,
            dst_ref=dst,
            send_sem=send,
            recv_sem=recv,
            device_id=where,
            device_id_type=MESH,
        )

    def z_copies(source, way, k):
        slot = source * 2 + x
        span = pl.ds(k * part, part)
        to = {"expert": me + 2 if way == 0 else me - 2}
        return (
            remote(
                tokens.at[slot, span], tokens.at[slot, span],
                zg_send.at[source, way, k], zg_recv.at[source, k], to,
            ),
            remote(
                hiddens.at[slot, span], hiddens.at[slot, span],
                zh_send.at[source, way, k], zh_recv.at[source, k], to,
            ),
        )

    def x_tokens(source, k, column):
        slot = source * 2 + column
        span = pl.ds(k * part, part)
        return remote(
            tokens.at[slot, span], tokens.at[slot, span],
            xg_send.at[source, k], xg_recv.at[source, k], {"expert": across},
        )

    def x_hidden(source, k):
        span = pl.ds(k * part, part)
        return remote(
            cross_out.at[source, span], cross_in.at[source, span],
            xh_send.at[source, k], xh_recv.at[source, k], {"expert": across},
        )

    def back_copy(slot):
        return remote(
            back_out.at[slot], back_in.at[me], back_send.at[slot], back_recv.at[me], {"expert": slot}
        )

    def meta_copy(slot):
        return remote(
            metas.at[me], metas.at[me], meta_send.at[slot], meta_recv.at[me], {"expert": slot}
        )

    def weight_copy():
        return remote(
            weight_ref, weight.at[pl.ds(low, half)], dp_send.at[0], dp_recv.at[0], {"dp": 1 - core}
        )

    def half_copy():
        return remote(half_out, half_in, dp_send.at[1], dp_recv.at[1], {"dp": 1 - core})

    def moves_up(source):
        return jnp.logical_and(source <= z, z < planes - 1)

    def moves_down(source):
        return jnp.logical_and(source >= z, z > 0)

    def each_peer(body):
        def step(slot, carry):
            @pl.when(slot != me)
            def _():
                body(slot)

            return carry

        lax.fori_loop(0, peers, step, 0)

    barrier = pltpu.get_barrier_semaphore()
    each_peer(
        lambda slot: pl.semaphore_signal(
            barrier, inc=1, device_id={"expert": slot}, device_id_type=MESH
        )
    )
    pl.semaphore_signal(barrier, inc=1, device_id={"dp": 1 - core}, device_id_type=MESH)

    metas[me] = meta_ref[...]
    tokens[me] = grad_ref[...]
    for route in range(2):
        base = route * 2 * units
        gate = pre_ref[:, base : base + units].astype(jnp.float32)
        up = pre_ref[:, base + units : base + 2 * units].astype(jnp.float32)
        hiddens[me, :, route * units : (route + 1) * units] = gate_hidden(gate, up)

    pl.semaphore_wait(barrier, peers)
    each_peer(lambda slot: meta_copy(slot).start())

    def pick(slot, k, expert):
        span = pl.ds(k * part, part)
        table = columns[slot, span]
        wanted = expert.astype(jnp.float32)
        first = hiddens[slot, span, :units].astype(jnp.float32)
        second = hiddens[slot, span, units:].astype(jnp.float32)
        rest = jnp.where(table[:, 1:2] == wanted, second, 0.0)
        return jnp.where(table[:, 0:1] == wanted, first, rest).astype(jnp.bfloat16)

    def forward_z(source, k):
        @pl.when(moves_up(source))
        def _():
            for copy in z_copies(source, 0, k):
                copy.start()

        @pl.when(moves_down(source))
        def _():
            for copy in z_copies(source, 1, k):
                copy.start()

    for k in range(CHUNKS):
        forward_z(z, k)
        x_tokens(z, k, x).start()
    weight_copy().start()
    weight[pl.ds(low, half)] = weight_ref[...]
    total[...] = jnp.zeros_like(total)
    columns[me] = jnp.transpose(metas[me])

    def take_meta(slot):
        remote(
            metas.at[slot], metas.at[slot], meta_send.at[slot], meta_recv.at[slot], {"expert": slot}
        ).wait_recv()
        columns[slot] = jnp.transpose(metas[slot])

    each_peer(take_meta)
    remote(
        weight_ref, weight.at[pl.ds(other, half)], dp_send.at[0], dp_recv.at[0], {"dp": 1 - core}
    ).wait_recv()

    def work(slot):
        table = columns[slot]
        wanted = me.astype(jnp.float32)
        factor = jnp.where(
            table[:, 0:1] == wanted,
            table[:, 2:3],
            jnp.where(table[:, 1:2] == wanted, table[:, 3:4], 0.0),
        )
        back_sum[...] = jnp.zeros_like(back_sum)

        def tile(j, carry):
            span = pl.ds(pl.multiple_of(j * TILE, TILE), TILE)
            scaled = (factor * tokens[slot, :, span].astype(jnp.float32)).astype(jnp.bfloat16)
            total[:, span] += lax.dot_general(
                chosen[...], scaled, (((0,), (0,)), ((), ())), preferred_element_type=jnp.float32
            )
            back_sum[...] += lax.dot_general(
                scaled, weight[:, span], (((1,), (1,)), ((), ())), preferred_element_type=jnp.float32
            )
            return carry

        lax.fori_loop(0, width // TILE, tile, 0)

        @pl.when(slot == me)
        def _():
            back_in[me] = back_sum[...].astype(jnp.bfloat16)

        @pl.when(slot != me)
        def _():
            back_out[slot] = back_sum[...].astype(jnp.bfloat16)
            back_copy(slot).start()

    def turn_step(turn, carry):
        @pl.when(turn < planes)
        def _():
            source = source_at(z, turn, planes)
            slot = source * 2 + x
            for k in range(CHUNKS):
                @pl.when(turn > 0)
                def _():
                    for copy in z_copies(source, 0, k):
                        copy.wait_recv()
                    forward_z(source, k)
                    x_tokens(source, k, x).start()

                span = pl.ds(k * part, part)
                cross_out[source, span] = pick(slot, k, across)
                x_hidden(source, k).start()

        def side(column, inner):
            @pl.when(jnp.logical_and(column == 0, turn < planes))
            def _():
                slot = source_at(z, turn, planes) * 2 + x
                for k in range(CHUNKS):
                    chosen[pl.ds(k * part, part)] = pick(slot, k, me)

            @pl.when(jnp.logical_and(column == 1, turn > 0))
            def _():
                source = source_at(z, turn - 1, planes)
                for k in range(CHUNKS):
                    x_tokens(source, k, 1 - x).wait_recv()
                    x_hidden(source, k).wait_recv()
                chosen[...] = cross_in[source]

            @pl.when(jnp.where(column == 0, turn < planes, turn > 0))
            def _():
                source = source_at(z, turn - column, planes)
                work(source * 2 + (x + column) % 2)

            return inner

        return lax.fori_loop(0, 2, side, carry)

    lax.fori_loop(0, planes + 1, turn_step, 0)

    half_out[...] = total[pl.ds(other, half)].astype(jnp.bfloat16)
    half_copy().start()

    each_peer(
        lambda slot: remote(
            back_out.at[slot], back_in.at[slot], back_send.at[slot], back_recv.at[slot],
            {"expert": slot},
        ).wait_recv()
    )
    mine = columns[me]
    for route in range(2):
        def gather(slot, carry):
            hit = mine[:, route : route + 1] == slot.astype(jnp.float32)
            back_sum[...] = jnp.where(hit, back_in[slot].astype(jnp.float32), back_sum[...])
            return carry

        lax.fori_loop(0, peers, gather, 0)
        base = route * 2 * units
        gate = pre_ref[:, base : base + units].astype(jnp.float32)
        up = pre_ref[:, base + units : base + 2 * units].astype(jnp.float32)
        d_pre_ref[:, base : base + 2 * units] = activation_grads(back_sum[...], gate, up)

    half_copy().wait_recv()
    kept = total[pl.ds(low, half)].astype(jnp.bfloat16).astype(jnp.float32)
    down_ref[...] = (kept + half_in[...].astype(jnp.float32)).astype(jnp.bfloat16)

    weight_copy().wait_send()
    half_copy().wait_send()

    def drain(slot):
        back_copy(slot).wait_send()
        meta_copy(slot).wait_send()

    each_peer(drain)

    def drain_plane(source, carry):
        for k in range(CHUNKS):
            x_tokens(source, k, x).wait_send()
            x_hidden(source, k).wait_send()

            @pl.when(moves_up(source))
            def _():
                for copy in z_copies(source, 0, k):
                    copy.wait_send()

            @pl.when(moves_down(source))
            def _():
                for copy in z_copies(source, 1, k):
                    copy.wait_send()

        return carry

    lax.fori_loop(0, planes, drain_plane, 0)


def dense_shards(grad_out, pre_act, routes, gate_prob, down_weight):
    peers = lax.axis_size("expert")
    planes = peers // 2
    rows, width = grad_out.shape
    units = pre_act.shape[3]
    half = down_weight.shape[1]
    meta = jnp.concatenate([routes.astype(jnp.float32), gate_prob], axis=1).T
    meta = jnp.concatenate([meta, jnp.zeros_like(meta)], axis=0)
    whole = pl.BlockSpec(memory_space=pltpu.VMEM)
    dma = pltpu.SemaphoreType.DMA
    bf16, f32 = jnp.bfloat16, jnp.float32
    d_pre, grad_down = pl.pallas_call(
        functools.partial(dense_kernel, peers),
        out_shape=(
            jax.ShapeDtypeStruct((rows, 4 * units), bf16),
            jax.ShapeDtypeStruct((half, width), bf16),
        ),
        in_specs=[whole] * 4,
        out_specs=(whole, whole),
        scratch_shapes=[
            pltpu.VMEM((peers, rows, width), bf16),
            pltpu.VMEM((peers, rows, 2 * units), bf16),
            pltpu.VMEM((planes, rows, units), bf16),
            pltpu.VMEM((planes, rows, units), bf16),
            pltpu.VMEM((peers, 8, rows), f32),
            pltpu.VMEM((peers, rows, 8), f32),
            pltpu.VMEM((units, width), bf16),
            pltpu.VMEM((rows, units), bf16),
            pltpu.VMEM((rows, units), f32),
            pltpu.VMEM((peers, rows, units), bf16),
            pltpu.VMEM((peers, rows, units), bf16),
            pltpu.VMEM((units, width), f32),
            pltpu.VMEM((half, width), bf16),
            pltpu.VMEM((half, width), bf16),
            dma((planes, 2, CHUNKS)),
            dma((planes, CHUNKS)),
            dma((planes, 2, CHUNKS)),
            dma((planes, CHUNKS)),
            dma((planes, CHUNKS)),
            dma((planes, CHUNKS)),
            dma((planes, CHUNKS)),
            dma((planes, CHUNKS)),
            dma((peers,)),
            dma((peers,)),
            dma((peers,)),
            dma((peers,)),
            dma((2,)),
            dma((2,)),
        ],
        compiler_params=pltpu.CompilerParams(
            collective_id=0, has_side_effects=True, vmem_limit_bytes=48 * 1024 * 1024
        ),
    )(grad_out, pre_act.reshape(rows, 4 * units), meta, down_weight[0])
    return (d_pre.reshape(rows, 2, 2, units), grad_down[None])


def shards(grad_out, pre_act, routes, gate_prob, down_weight):
    peers, cores = lax.axis_size("expert"), lax.axis_size("dp")
    capacity = 4 * routes.shape[0] * routes.shape[1] // peers
    dense = capacity >= routes.shape[0] and peers % 2 == 0 and cores == 2
    plan = dense_shards if dense else packed_shards
    return plan(grad_out, pre_act, routes, gate_prob, down_weight)


def solution(mesh):
    placed = (
        P(("groups", "expert", "dp"), None),
        P(("groups", "expert", "dp"), None, None, None),
        P(("groups", "expert", "dp"), None),
        P(("groups", "expert", "dp"), None),
        P("expert", "dp", None),
    )
    return jax.shard_map(
        shards,
        mesh=mesh,
        in_specs=placed,
        out_specs=(
            P(("groups", "expert", "dp"), None, None, None),
            P(("groups", "expert"), "dp", None),
        ),
        check_vma=False,
    )
```

```python
import functools

import jax
import jax.numpy as jnp
from jax import lax
from jax.experimental import pallas as pl
from jax.experimental.pallas import tpu as pltpu
from jax.sharding import PartitionSpec as P


def gate_hidden(gate_pre, up_pre):
    sigmoid_gate = jax.nn.sigmoid(gate_pre)
    return (gate_pre * sigmoid_gate * up_pre).astype(jnp.bfloat16)


def activation_grads(hidden_grad, gate_pre, up_pre):
    sigmoid_gate = jax.nn.sigmoid(gate_pre)
    upstream = hidden_grad.astype(jnp.float32)
    gate_part = upstream * up_pre * sigmoid_gate * (1.0 + gate_pre * (1.0 - sigmoid_gate))
    up_part = upstream * (gate_pre * sigmoid_gate)
    return jnp.concatenate([gate_part, up_part], axis=-1).astype(jnp.bfloat16)


def pack_rows(row_values, slot_index, peer_count, capacity):
    row_width = row_values.shape[1]
    buffer = (
        jnp.zeros((peer_count * capacity, row_width), row_values.dtype)
        .at[slot_index]
        .set(row_values)
    )
    return buffer.reshape(peer_count, capacity, row_width)


def expert_work(scaled_rows, hidden_rows, full_weight):
    dims_back = (((1,), (1,)), ((), ()))
    dims_outer = (((0,), (0,)), ((), ()))
    hidden_grad = lax.dot_general(
        scaled_rows, full_weight, dims_back, preferred_element_type=jnp.float32
    ).astype(jnp.bfloat16)
    partial_value = lax.dot_general(
        hidden_rows, scaled_rows, dims_outer, preferred_element_type=jnp.float32
    )
    return (hidden_grad, partial_value)


def balanced_work(got_scaled, got_hidden, full_weight):
    peer_count = got_scaled.shape[0]
    capacity = got_scaled.shape[1]
    slots_all = peer_count * capacity
    scaled_rows = got_scaled.reshape(slots_all, got_scaled.shape[2])
    hidden_rows = got_hidden.reshape(slots_all, got_hidden.shape[2])
    hidden_grad, partial_value = expert_work(scaled_rows, hidden_rows, full_weight)
    return (hidden_grad.reshape(peer_count, capacity, hidden_grad.shape[1]), partial_value)


def packed_shards(grad_out, pre_act, routes, gate_prob, down_weight):
    peer_count = lax.axis_size("expert")
    token_rows = routes.shape[0]
    route_width = routes.shape[1]
    route_count = token_rows * route_width
    capacity = 4 * route_count // peer_count
    feature_count = grad_out.shape[1]
    hidden_count = pre_act.shape[3]
    scaled = (
        (gate_prob[:, :, None] * grad_out[:, None, :].astype(jnp.float32))
        .astype(jnp.bfloat16)
        .reshape(route_count, feature_count)
    )
    pre_rows = pre_act.reshape(route_count, 2 * hidden_count)
    expert_ids = routes.reshape(route_count)
    one_hot = (expert_ids[:, None] == jnp.arange(peer_count, dtype=jnp.int32)[None, :]).astype(
        jnp.int32
    )
    slot_rank = jnp.sum(jnp.cumsum(one_hot, axis=0) * one_hot, axis=1) - 1
    sent_counts = jnp.sum(one_hot, axis=0).reshape(peer_count, 1)
    slot_index = expert_ids * capacity + slot_rank
    full_weight = lax.all_gather(down_weight[0], "dp", axis=0, tiled=True)
    got_scaled, got_pre, arrived = (
        lax.all_to_all(
            pack_rows(scaled, slot_index, peer_count, capacity),
            "expert",
            split_axis=0,
            concat_axis=0,
            tiled=True,
        ),
        lax.all_to_all(
            pack_rows(pre_rows, slot_index, peer_count, capacity),
            "expert",
            split_axis=0,
            concat_axis=0,
            tiled=True,
        ),
        lax.all_to_all(sent_counts, "expert", split_axis=0, concat_axis=0, tiled=True),
    )
    pre_float = got_pre.astype(jnp.float32)
    gate_pre = pre_float[:, :, :hidden_count]
    up_pre = pre_float[:, :, hidden_count:]
    got_hidden = gate_hidden(gate_pre, up_pre)
    hidden_grad, partial_value = balanced_work(got_scaled, got_hidden, full_weight)
    slot_grads = activation_grads(hidden_grad, gate_pre, up_pre)
    returned = lax.all_to_all(slot_grads, "expert", split_axis=0, concat_axis=0, tiled=True)
    d_pre = returned.reshape(peer_count * capacity, 2 * hidden_count)[slot_index]
    summed = lax.psum_scatter(
        partial_value.astype(jnp.bfloat16), "dp", scatter_dimension=0, tiled=True
    )
    return (d_pre.reshape(token_rows, route_width, 2, hidden_count), summed[None])


CHUNKS = 4
TILE = 512
MESH = pl.DeviceIdType.MESH


def source_at(z, turn, planes):
    reach = jnp.minimum(z, planes - 1 - z)
    step = (turn + 1) // 2
    near = jnp.where(turn % 2 == 1, z - step, z + step)
    far = jnp.where(2 * z <= planes - 1, turn, planes - 1 - turn)
    return jnp.where(turn <= 2 * reach, near, far)


def dense_kernel(
    peers,
    grad_ref,
    pre_ref,
    routes_ref,
    prob_ref,
    weight_ref,
    d_pre_ref,
    down_ref,
    tokens,
    hiddens,
    cross_out,
    cross_in,
    metas,
    columns,
    weight,
    chosen,
    back_sum,
    back_out,
    back_in,
    total,
    half_out,
    half_in,
    zg_send,
    zg_recv,
    zh_send,
    zh_recv,
    xg_send,
    xg_recv,
    xh_send,
    xh_recv,
    back_send,
    back_recv,
    meta_send,
    meta_recv,
    dp_send,
    dp_recv,
    load_sem,
):
    planes = peers // 2
    me = lax.axis_index("expert")
    core = lax.axis_index("dp")
    z, x = me // 2, me % 2
    across = z * 2 + 1 - x
    rows, width = grad_ref.shape
    units = weight.shape[0]
    half = units // 2
    part = rows // CHUNKS
    low = pl.multiple_of(core * half, half)
    other = pl.multiple_of((1 - core) * half, half)

    def remote(src, dst, send, recv, where):
        return pltpu.make_async_remote_copy(
            src_ref=src,
            dst_ref=dst,
            send_sem=send,
            recv_sem=recv,
            device_id=where,
            device_id_type=MESH,
        )

    def z_copies(source, way, k):
        slot = source * 2 + x
        span = pl.ds(k * part, part)
        to = {"expert": me + 2 if way == 0 else me - 2}
        return (
            remote(
                tokens.at[slot, span], tokens.at[slot, span],
                zg_send.at[source, way, k], zg_recv.at[source, k], to,
            ),
            remote(
                hiddens.at[slot, span], hiddens.at[slot, span],
                zh_send.at[source, way, k], zh_recv.at[source, k], to,
            ),
        )

    def x_tokens(source, k, column):
        slot = source * 2 + column
        span = pl.ds(k * part, part)
        return remote(
            tokens.at[slot, span], tokens.at[slot, span],
            xg_send.at[source, k], xg_recv.at[source, k], {"expert": across},
        )

    def x_hidden(source, k):
        span = pl.ds(k * part, part)
        return remote(
            cross_out.at[source, span], cross_in.at[source, span],
            xh_send.at[source, k], xh_recv.at[source, k], {"expert": across},
        )

    def back_copy(slot):
        return remote(
            back_out.at[slot], back_in.at[me], back_send.at[slot], back_recv.at[me], {"expert": slot}
        )

    def meta_copy(slot):
        return remote(
            metas.at[me], metas.at[me], meta_send.at[slot], meta_recv.at[me], {"expert": slot}
        )

    def weight_copy():
        return remote(
            weight.at[pl.ds(low, half)], weight.at[pl.ds(low, half)], dp_send.at[0], dp_recv.at[0], {"dp": 1 - core}
        )

    def half_copy():
        return remote(half_out, half_in, dp_send.at[1], dp_recv.at[1], {"dp": 1 - core})

    def moves_up(source):
        return jnp.logical_and(source <= z, z < planes - 1)

    def moves_down(source):
        return jnp.logical_and(source >= z, z > 0)

    def each_peer(body):
        def step(slot, carry):
            @pl.when(slot != me)
            def _():
                body(slot)

            return carry

        lax.fori_loop(0, peers, step, 0)

    barrier = pltpu.get_barrier_semaphore()
    each_peer(
        lambda slot: pl.semaphore_signal(
            barrier, inc=1, device_id={"expert": slot}, device_id_type=MESH
        )
    )
    pl.semaphore_signal(barrier, inc=1, device_id={"dp": 1 - core}, device_id_type=MESH)

    metas[me] = jnp.zeros((8, rows), jnp.float32)
    metas[me, 0:2] = routes_ref[...].astype(jnp.float32)
    metas[me, 2:4] = prob_ref[...]
    load_tokens = pltpu.make_async_copy(grad_ref, tokens.at[me], load_sem.at[0])
    load_tokens.start()
    load_weight = pltpu.make_async_copy(
        weight_ref, weight.at[pl.ds(low, half)], load_sem.at[1]
    )
    load_weight.start()
    for route in range(2):
        base = route * 2 * units
        gate = pre_ref[:, base : base + units].astype(jnp.float32)
        up = pre_ref[:, base + units : base + 2 * units].astype(jnp.float32)
        hiddens[me, :, route * units : (route + 1) * units] = gate_hidden(gate, up)

    pl.semaphore_wait(barrier, peers)
    load_tokens.wait()
    each_peer(lambda slot: meta_copy(slot).start())

    def pick(slot, k, expert):
        span = pl.ds(k * part, part)
        table = columns[slot, span]
        wanted = expert.astype(jnp.float32)
        first = hiddens[slot, span, :units].astype(jnp.float32)
        second = hiddens[slot, span, units:].astype(jnp.float32)
        rest = jnp.where(table[:, 1:2] == wanted, second, 0.0)
        return jnp.where(table[:, 0:1] == wanted, first, rest).astype(jnp.bfloat16)

    def forward_z(source, k):
        @pl.when(moves_up(source))
        def _():
            for copy in z_copies(source, 0, k):
                copy.start()

        @pl.when(moves_down(source))
        def _():
            for copy in z_copies(source, 1, k):
                copy.start()

    for k in range(CHUNKS):
        forward_z(z, k)
        x_tokens(z, k, x).start()
    load_weight.wait()
    weight_copy().start()
    total[...] = jnp.zeros_like(total)
    columns[me] = jnp.transpose(metas[me])

    def take_meta(slot):
        remote(
            metas.at[slot], metas.at[slot], meta_send.at[slot], meta_recv.at[slot], {"expert": slot}
        ).wait_recv()
        columns[slot] = jnp.transpose(metas[slot])

    each_peer(take_meta)
    remote(
        weight.at[pl.ds(other, half)], weight.at[pl.ds(other, half)], dp_send.at[0], dp_recv.at[0], {"dp": 1 - core}
    ).wait_recv()

    def work(slot, now):
        table = columns[slot]
        wanted = me.astype(jnp.float32)
        factor = jnp.where(
            table[:, 0:1] == wanted,
            table[:, 2:3],
            jnp.where(table[:, 1:2] == wanted, table[:, 3:4], 0.0),
        )
        back_sum[...] = jnp.zeros_like(back_sum)

        def tile(j, carry):
            span = pl.ds(pl.multiple_of(j * TILE, TILE), TILE)
            scaled = (factor * tokens[slot, :, span].astype(jnp.float32)).astype(jnp.bfloat16)
            total[:, span] += lax.dot_general(
                chosen[...], scaled, (((0,), (0,)), ((), ())), preferred_element_type=jnp.float32
            )
            back_sum[...] += lax.dot_general(
                scaled, weight[:, span], (((1,), (1,)), ((), ())), preferred_element_type=jnp.float32
            )
            return carry

        lax.fori_loop(0, width // TILE, tile, 0)

        @pl.when(slot == me)
        def _():
            back_in[me] = back_sum[...].astype(jnp.bfloat16)

        @pl.when(slot != me)
        def _():
            back_out[slot] = back_sum[...].astype(jnp.bfloat16)

            @pl.when(now)
            def _():
                back_copy(slot).start()

    def turn_step(turn, carry):
        @pl.when(turn < planes)
        def _():
            source = source_at(z, turn, planes)
            slot = source * 2 + x
            for k in range(CHUNKS):
                @pl.when(turn > 0)
                def _():
                    for copy in z_copies(source, 0, k):
                        copy.wait_recv()
                    forward_z(source, k)
                    x_tokens(source, k, x).start()

                span = pl.ds(k * part, part)
                cross_out[source, span] = pick(slot, k, across)
                x_hidden(source, k).start()

        @pl.when(turn == planes - 1)
        def _():
            def release(index, carry):
                slot = source_at(z, index // 2, planes) * 2 + (x + index % 2) % 2

                @pl.when(slot != me)
                def _():
                    back_copy(slot).start()

                return carry

            lax.fori_loop(0, 2 * planes - 3, release, 0)

        def side(column, inner):
            @pl.when(jnp.logical_and(column == 0, turn < planes))
            def _():
                slot = source_at(z, turn, planes) * 2 + x
                for k in range(CHUNKS):
                    chosen[pl.ds(k * part, part)] = pick(slot, k, me)

            @pl.when(jnp.logical_and(column == 1, turn > 0))
            def _():
                source = source_at(z, turn - 1, planes)
                for k in range(CHUNKS):
                    x_tokens(source, k, 1 - x).wait_recv()
                    x_hidden(source, k).wait_recv()
                chosen[...] = cross_in[source]

            @pl.when(jnp.where(column == 0, turn < planes, turn > 0))
            def _():
                source = source_at(z, turn - column, planes)
                work(source * 2 + (x + column) % 2, turn >= planes - 1)

            return inner

        return lax.fori_loop(0, 2, side, carry)

    lax.fori_loop(0, planes + 1, turn_step, 0)

    half_out[...] = total[pl.ds(other, half)].astype(jnp.bfloat16)
    half_copy().start()

    each_peer(
        lambda slot: remote(
            back_out.at[slot], back_in.at[slot], back_send.at[slot], back_recv.at[slot],
            {"expert": slot},
        ).wait_recv()
    )
    mine = columns[me]
    for route in range(2):
        def gather(slot, carry):
            hit = mine[:, route : route + 1] == slot.astype(jnp.float32)
            back_sum[...] = jnp.where(hit, back_in[slot].astype(jnp.float32), back_sum[...])
            return carry

        lax.fori_loop(0, peers, gather, 0)
        base = route * 2 * units
        gate = pre_ref[:, base : base + units].astype(jnp.float32)
        up = pre_ref[:, base + units : base + 2 * units].astype(jnp.float32)
        d_pre_ref[:, base : base + 2 * units] = activation_grads(back_sum[...], gate, up)

    half_copy().wait_recv()
    kept = total[pl.ds(low, half)].astype(jnp.bfloat16).astype(jnp.float32)
    down_ref[...] = (kept + half_in[...].astype(jnp.float32)).astype(jnp.bfloat16)

    weight_copy().wait_send()
    half_copy().wait_send()

    def drain(slot):
        back_copy(slot).wait_send()
        meta_copy(slot).wait_send()

    each_peer(drain)

    def drain_plane(source, carry):
        for k in range(CHUNKS):
            x_tokens(source, k, x).wait_send()
            x_hidden(source, k).wait_send()

            @pl.when(moves_up(source))
            def _():
                for copy in z_copies(source, 0, k):
                    copy.wait_send()

            @pl.when(moves_down(source))
            def _():
                for copy in z_copies(source, 1, k):
                    copy.wait_send()

        return carry

    lax.fori_loop(0, planes, drain_plane, 0)


def dense_shards(grad_out, pre_act, routes, gate_prob, down_weight):
    peers = lax.axis_size("expert")
    planes = peers // 2
    rows, width = grad_out.shape
    units = pre_act.shape[3]
    half = down_weight.shape[1]
    whole = pl.BlockSpec(memory_space=pltpu.VMEM)
    away = pl.BlockSpec(memory_space=pl.ANY)
    dma = pltpu.SemaphoreType.DMA
    bf16, f32 = jnp.bfloat16, jnp.float32
    d_pre, grad_down = pl.pallas_call(
        functools.partial(dense_kernel, peers),
        out_shape=(
            jax.ShapeDtypeStruct((rows, 4 * units), bf16),
            jax.ShapeDtypeStruct((half, width), bf16),
        ),
        in_specs=[away, whole, whole, whole, away],
        out_specs=(whole, whole),
        scratch_shapes=[
            pltpu.VMEM((peers, rows, width), bf16),
            pltpu.VMEM((peers, rows, 2 * units), bf16),
            pltpu.VMEM((planes, rows, units), bf16),
            pltpu.VMEM((planes, rows, units), bf16),
            pltpu.VMEM((peers, 8, rows), f32),
            pltpu.VMEM((peers, rows, 8), f32),
            pltpu.VMEM((units, width), bf16),
            pltpu.VMEM((rows, units), bf16),
            pltpu.VMEM((rows, units), f32),
            pltpu.VMEM((peers, rows, units), bf16),
            pltpu.VMEM((peers, rows, units), bf16),
            pltpu.VMEM((units, width), f32),
            pltpu.VMEM((half, width), bf16),
            pltpu.VMEM((half, width), bf16),
            dma((planes, 2, CHUNKS)),
            dma((planes, CHUNKS)),
            dma((planes, 2, CHUNKS)),
            dma((planes, CHUNKS)),
            dma((planes, CHUNKS)),
            dma((planes, CHUNKS)),
            dma((planes, CHUNKS)),
            dma((planes, CHUNKS)),
            dma((peers,)),
            dma((peers,)),
            dma((peers,)),
            dma((peers,)),
            dma((2,)),
            dma((2,)),
            dma((2,)),
        ],
        compiler_params=pltpu.CompilerParams(
            collective_id=0, has_side_effects=True, vmem_limit_bytes=48 * 1024 * 1024
        ),
    )(grad_out, pre_act.reshape(rows, 4 * units), routes.T, gate_prob.T, down_weight[0])
    return (d_pre.reshape(rows, 2, 2, units), grad_down[None])


def shards(grad_out, pre_act, routes, gate_prob, down_weight):
    peers, cores = lax.axis_size("expert"), lax.axis_size("dp")
    capacity = 4 * routes.shape[0] * routes.shape[1] // peers
    dense = capacity >= routes.shape[0] and peers % 2 == 0 and cores == 2
    plan = dense_shards if dense else packed_shards
    return plan(grad_out, pre_act, routes, gate_prob, down_weight)


def solution(mesh):
    placed = (
        P(("groups", "expert", "dp"), None),
        P(("groups", "expert", "dp"), None, None, None),
        P(("groups", "expert", "dp"), None),
        P(("groups", "expert", "dp"), None),
        P("expert", "dp", None),
    )
    return jax.shard_map(
        shards,
        mesh=mesh,
        in_specs=placed,
        out_specs=(
            P(("groups", "expert", "dp"), None, None, None),
            P(("groups", "expert"), "dp", None),
        ),
        check_vma=False,
    )
```

```python
import functools

import jax
import jax.numpy as jnp
from jax import lax
from jax.experimental import pallas as pl
from jax.experimental.pallas import tpu as pltpu
from jax.sharding import PartitionSpec as P


def gate_hidden(gate_pre, up_pre):
    sigmoid_gate = jax.nn.sigmoid(gate_pre)
    return (gate_pre * sigmoid_gate * up_pre).astype(jnp.bfloat16)


def activation_grads(hidden_grad, gate_pre, up_pre):
    sigmoid_gate = jax.nn.sigmoid(gate_pre)
    upstream = hidden_grad.astype(jnp.float32)
    gate_part = upstream * up_pre * sigmoid_gate * (1.0 + gate_pre * (1.0 - sigmoid_gate))
    up_part = upstream * (gate_pre * sigmoid_gate)
    return jnp.concatenate([gate_part, up_part], axis=-1).astype(jnp.bfloat16)


def pack_rows(row_values, slot_index, peer_count, capacity):
    row_width = row_values.shape[1]
    buffer = (
        jnp.zeros((peer_count * capacity, row_width), row_values.dtype)
        .at[slot_index]
        .set(row_values)
    )
    return buffer.reshape(peer_count, capacity, row_width)


def expert_work(scaled_rows, hidden_rows, full_weight):
    dims_back = (((1,), (1,)), ((), ()))
    dims_outer = (((0,), (0,)), ((), ()))
    hidden_grad = lax.dot_general(
        scaled_rows, full_weight, dims_back, preferred_element_type=jnp.float32
    ).astype(jnp.bfloat16)
    partial_value = lax.dot_general(
        hidden_rows, scaled_rows, dims_outer, preferred_element_type=jnp.float32
    )
    return (hidden_grad, partial_value)


def balanced_work(got_scaled, got_hidden, full_weight):
    peer_count = got_scaled.shape[0]
    capacity = got_scaled.shape[1]
    slots_all = peer_count * capacity
    scaled_rows = got_scaled.reshape(slots_all, got_scaled.shape[2])
    hidden_rows = got_hidden.reshape(slots_all, got_hidden.shape[2])
    hidden_grad, partial_value = expert_work(scaled_rows, hidden_rows, full_weight)
    return (hidden_grad.reshape(peer_count, capacity, hidden_grad.shape[1]), partial_value)


def packed_shards(grad_out, pre_act, routes, gate_prob, down_weight):
    peer_count = lax.axis_size("expert")
    token_rows = routes.shape[0]
    route_width = routes.shape[1]
    route_count = token_rows * route_width
    capacity = 4 * route_count // peer_count
    feature_count = grad_out.shape[1]
    hidden_count = pre_act.shape[3]
    scaled = (
        (gate_prob[:, :, None] * grad_out[:, None, :].astype(jnp.float32))
        .astype(jnp.bfloat16)
        .reshape(route_count, feature_count)
    )
    pre_rows = pre_act.reshape(route_count, 2 * hidden_count)
    expert_ids = routes.reshape(route_count)
    one_hot = (expert_ids[:, None] == jnp.arange(peer_count, dtype=jnp.int32)[None, :]).astype(
        jnp.int32
    )
    slot_rank = jnp.sum(jnp.cumsum(one_hot, axis=0) * one_hot, axis=1) - 1
    sent_counts = jnp.sum(one_hot, axis=0).reshape(peer_count, 1)
    slot_index = expert_ids * capacity + slot_rank
    full_weight = lax.all_gather(down_weight[0], "dp", axis=0, tiled=True)
    got_scaled, got_pre, arrived = (
        lax.all_to_all(
            pack_rows(scaled, slot_index, peer_count, capacity),
            "expert",
            split_axis=0,
            concat_axis=0,
            tiled=True,
        ),
        lax.all_to_all(
            pack_rows(pre_rows, slot_index, peer_count, capacity),
            "expert",
            split_axis=0,
            concat_axis=0,
            tiled=True,
        ),
        lax.all_to_all(sent_counts, "expert", split_axis=0, concat_axis=0, tiled=True),
    )
    pre_float = got_pre.astype(jnp.float32)
    gate_pre = pre_float[:, :, :hidden_count]
    up_pre = pre_float[:, :, hidden_count:]
    got_hidden = gate_hidden(gate_pre, up_pre)
    hidden_grad, partial_value = balanced_work(got_scaled, got_hidden, full_weight)
    slot_grads = activation_grads(hidden_grad, gate_pre, up_pre)
    returned = lax.all_to_all(slot_grads, "expert", split_axis=0, concat_axis=0, tiled=True)
    d_pre = returned.reshape(peer_count * capacity, 2 * hidden_count)[slot_index]
    summed = lax.psum_scatter(
        partial_value.astype(jnp.bfloat16), "dp", scatter_dimension=0, tiled=True
    )
    return (d_pre.reshape(token_rows, route_width, 2, hidden_count), summed[None])


CHUNKS = 4
TILE = 512
MESH = pl.DeviceIdType.MESH


def source_at(z, turn, planes):
    reach = jnp.minimum(z, planes - 1 - z)
    step = (turn + 1) // 2
    lower = 2 * z <= planes - 1
    odd = jnp.where(turn % 2 == 1, 1, -1)
    near = jnp.where(lower, z + odd * step, z - odd * step)
    far = jnp.where(lower, turn, planes - 1 - turn)
    return jnp.where(turn <= 2 * reach, near, far)


def dense_kernel(
    peers,
    grad_ref,
    pre_ref,
    routes_ref,
    prob_ref,
    weight_ref,
    d_pre_ref,
    down_ref,
    tokens,
    hiddens,
    cross_out,
    cross_in,
    metas,
    columns,
    weight,
    chosen,
    back_sum,
    back_out,
    back_in,
    total,
    half_out,
    half_in,
    zg_send,
    zg_recv,
    zh_send,
    zh_recv,
    xg_send,
    xg_recv,
    xh_send,
    xh_recv,
    back_send,
    back_recv,
    meta_send,
    meta_recv,
    dp_send,
    dp_recv,
    load_sem,
):
    planes = peers // 2
    me = lax.axis_index("expert")
    core = lax.axis_index("dp")
    z, x = me // 2, me % 2
    across = z * 2 + 1 - x
    rows, width = grad_ref.shape
    units = weight.shape[0]
    half = units // 2
    part = rows // CHUNKS
    low = pl.multiple_of(core * half, half)
    other = pl.multiple_of((1 - core) * half, half)

    def remote(src, dst, send, recv, where):
        return pltpu.make_async_remote_copy(
            src_ref=src,
            dst_ref=dst,
            send_sem=send,
            recv_sem=recv,
            device_id=where,
            device_id_type=MESH,
        )

    def z_copies(source, way, k):
        slot = source * 2 + x
        span = pl.ds(k * part, part)
        to = {"expert": me + 2 if way == 0 else me - 2}
        return (
            remote(
                tokens.at[slot, span], tokens.at[slot, span],
                zg_send.at[source, way, k], zg_recv.at[source, k], to,
            ),
            remote(
                hiddens.at[slot, span], hiddens.at[slot, span],
                zh_send.at[source, way, k], zh_recv.at[source, k], to,
            ),
        )

    def x_tokens(source, k, column):
        slot = source * 2 + column
        span = pl.ds(k * part, part)
        return remote(
            tokens.at[slot, span], tokens.at[slot, span],
            xg_send.at[source, k], xg_recv.at[source, k], {"expert": across},
        )

    def x_hidden(source, k):
        span = pl.ds(k * part, part)
        return remote(
            cross_out.at[source, span], cross_in.at[source, span],
            xh_send.at[source, k], xh_recv.at[source, k], {"expert": across},
        )

    def back_copy(slot):
        return remote(
            back_out.at[slot], back_in.at[me], back_send.at[slot], back_recv.at[me], {"expert": slot}
        )

    def meta_copy(slot):
        return remote(
            metas.at[me], metas.at[me], meta_send.at[slot], meta_recv.at[me], {"expert": slot}
        )

    def weight_copy():
        return remote(
            weight.at[pl.ds(low, half)], weight.at[pl.ds(low, half)], dp_send.at[0], dp_recv.at[0], {"dp": 1 - core}
        )

    def half_copy():
        return remote(half_out, half_in, dp_send.at[1], dp_recv.at[1], {"dp": 1 - core})

    def moves_up(source):
        return jnp.logical_and(source <= z, z < planes - 1)

    def moves_down(source):
        return jnp.logical_and(source >= z, z > 0)

    def each_peer(body):
        def step(slot, carry):
            @pl.when(slot != me)
            def _():
                body(slot)

            return carry

        lax.fori_loop(0, peers, step, 0)

    barrier = pltpu.get_barrier_semaphore()
    each_peer(
        lambda slot: pl.semaphore_signal(
            barrier, inc=1, device_id={"expert": slot}, device_id_type=MESH
        )
    )
    pl.semaphore_signal(barrier, inc=1, device_id={"dp": 1 - core}, device_id_type=MESH)

    metas[me] = jnp.zeros((8, rows), jnp.float32)
    metas[me, 0:2] = routes_ref[...].astype(jnp.float32)
    metas[me, 2:4] = prob_ref[...]
    load_tokens = pltpu.make_async_copy(grad_ref, tokens.at[me], load_sem.at[0])
    load_tokens.start()
    load_weight = pltpu.make_async_copy(
        weight_ref, weight.at[pl.ds(low, half)], load_sem.at[1]
    )
    load_weight.start()
    for route in range(2):
        base = route * 2 * units
        gate = pre_ref[:, base : base + units].astype(jnp.float32)
        up = pre_ref[:, base + units : base + 2 * units].astype(jnp.float32)
        hiddens[me, :, route * units : (route + 1) * units] = gate_hidden(gate, up)

    pl.semaphore_wait(barrier, peers)
    load_tokens.wait()
    each_peer(lambda slot: meta_copy(slot).start())

    def pick(slot, k, expert):
        span = pl.ds(k * part, part)
        table = columns[slot, span]
        wanted = expert.astype(jnp.float32)
        first = hiddens[slot, span, :units].astype(jnp.float32)
        second = hiddens[slot, span, units:].astype(jnp.float32)
        rest = jnp.where(table[:, 1:2] == wanted, second, 0.0)
        return jnp.where(table[:, 0:1] == wanted, first, rest).astype(jnp.bfloat16)

    def forward_z(source, k):
        @pl.when(moves_up(source))
        def _():
            for copy in z_copies(source, 0, k):
                copy.start()

        @pl.when(moves_down(source))
        def _():
            for copy in z_copies(source, 1, k):
                copy.start()

    for k in range(CHUNKS):
        forward_z(z, k)
        x_tokens(z, k, x).start()
    load_weight.wait()
    weight_copy().start()
    total[...] = jnp.zeros_like(total)
    columns[me] = jnp.transpose(metas[me])

    def take_meta(slot):
        remote(
            metas.at[slot], metas.at[slot], meta_send.at[slot], meta_recv.at[slot], {"expert": slot}
        ).wait_recv()
        columns[slot] = jnp.transpose(metas[slot])

    each_peer(take_meta)
    remote(
        weight.at[pl.ds(other, half)], weight.at[pl.ds(other, half)], dp_send.at[0], dp_recv.at[0], {"dp": 1 - core}
    ).wait_recv()

    def work(slot, now):
        table = columns[slot]
        wanted = me.astype(jnp.float32)
        factor = jnp.where(
            table[:, 0:1] == wanted,
            table[:, 2:3],
            jnp.where(table[:, 1:2] == wanted, table[:, 3:4], 0.0),
        )
        back_sum[...] = jnp.zeros_like(back_sum)

        def tile(j, carry):
            span = pl.ds(pl.multiple_of(j * TILE, TILE), TILE)
            scaled = (factor * tokens[slot, :, span].astype(jnp.float32)).astype(jnp.bfloat16)
            total[:, span] += lax.dot_general(
                chosen[...], scaled, (((0,), (0,)), ((), ())), preferred_element_type=jnp.float32
            )
            back_sum[...] += lax.dot_general(
                scaled, weight[:, span], (((1,), (1,)), ((), ())), preferred_element_type=jnp.float32
            )
            return carry

        lax.fori_loop(0, width // TILE, tile, 0)

        @pl.when(slot == me)
        def _():
            back_in[me] = back_sum[...].astype(jnp.bfloat16)

        @pl.when(slot != me)
        def _():
            back_out[slot] = back_sum[...].astype(jnp.bfloat16)

            @pl.when(now)
            def _():
                back_copy(slot).start()

    edge = jnp.logical_or(z == 0, z == planes - 1)

    def now_at(turn):
        return jnp.logical_or(edge, turn >= planes - 1)

    def turn_step(turn, carry):
        @pl.when(turn < planes)
        def _():
            source = source_at(z, turn, planes)
            slot = source * 2 + x
            for k in range(CHUNKS):
                @pl.when(turn > 0)
                def _():
                    for copy in z_copies(source, 0, k):
                        copy.wait_recv()
                    forward_z(source, k)
                    x_tokens(source, k, x).start()

                span = pl.ds(k * part, part)
                cross_out[source, span] = pick(slot, k, across)
                x_hidden(source, k).start()

        @pl.when(jnp.logical_and(turn == planes - 1, jnp.logical_not(edge)))
        def _():
            def release(index, carry):
                slot = source_at(z, index // 2, planes) * 2 + (x + index % 2) % 2

                @pl.when(slot != me)
                def _():
                    back_copy(slot).start()

                return carry

            lax.fori_loop(0, 2 * planes - 3, release, 0)

        def side(column, inner):
            @pl.when(jnp.logical_and(column == 0, turn < planes))
            def _():
                slot = source_at(z, turn, planes) * 2 + x
                for k in range(CHUNKS):
                    chosen[pl.ds(k * part, part)] = pick(slot, k, me)

            @pl.when(jnp.logical_and(column == 1, turn > 0))
            def _():
                source = source_at(z, turn - 1, planes)
                for k in range(CHUNKS):
                    x_tokens(source, k, 1 - x).wait_recv()
                    x_hidden(source, k).wait_recv()
                chosen[...] = cross_in[source]

            @pl.when(jnp.where(column == 0, turn < planes, turn > 0))
            def _():
                source = source_at(z, turn - column, planes)
                work(source * 2 + (x + column) % 2, now_at(turn))

            return inner

        return lax.fori_loop(0, 2, side, carry)

    lax.fori_loop(0, planes + 1, turn_step, 0)

    half_out[...] = total[pl.ds(other, half)].astype(jnp.bfloat16)
    half_copy().start()

    each_peer(
        lambda slot: remote(
            back_out.at[slot], back_in.at[slot], back_send.at[slot], back_recv.at[slot],
            {"expert": slot},
        ).wait_recv()
    )
    mine = columns[me]
    for route in range(2):
        def gather(slot, carry):
            hit = mine[:, route : route + 1] == slot.astype(jnp.float32)
            back_sum[...] = jnp.where(hit, back_in[slot].astype(jnp.float32), back_sum[...])
            return carry

        lax.fori_loop(0, peers, gather, 0)
        base = route * 2 * units
        gate = pre_ref[:, base : base + units].astype(jnp.float32)
        up = pre_ref[:, base + units : base + 2 * units].astype(jnp.float32)
        d_pre_ref[:, base : base + 2 * units] = activation_grads(back_sum[...], gate, up)

    half_copy().wait_recv()
    kept = total[pl.ds(low, half)].astype(jnp.bfloat16).astype(jnp.float32)
    down_ref[...] = (kept + half_in[...].astype(jnp.float32)).astype(jnp.bfloat16)

    weight_copy().wait_send()
    half_copy().wait_send()

    def drain(slot):
        back_copy(slot).wait_send()
        meta_copy(slot).wait_send()

    each_peer(drain)

    def drain_plane(source, carry):
        for k in range(CHUNKS):
            x_tokens(source, k, x).wait_send()
            x_hidden(source, k).wait_send()

            @pl.when(moves_up(source))
            def _():
                for copy in z_copies(source, 0, k):
                    copy.wait_send()

            @pl.when(moves_down(source))
            def _():
                for copy in z_copies(source, 1, k):
                    copy.wait_send()

        return carry

    lax.fori_loop(0, planes, drain_plane, 0)


def dense_shards(grad_out, pre_act, routes, gate_prob, down_weight):
    peers = lax.axis_size("expert")
    planes = peers // 2
    rows, width = grad_out.shape
    units = pre_act.shape[3]
    half = down_weight.shape[1]
    whole = pl.BlockSpec(memory_space=pltpu.VMEM)
    away = pl.BlockSpec(memory_space=pl.ANY)
    dma = pltpu.SemaphoreType.DMA
    bf16, f32 = jnp.bfloat16, jnp.float32
    d_pre, grad_down = pl.pallas_call(
        functools.partial(dense_kernel, peers),
        out_shape=(
            jax.ShapeDtypeStruct((rows, 4 * units), bf16),
            jax.ShapeDtypeStruct((half, width), bf16),
        ),
        in_specs=[away, whole, whole, whole, away],
        out_specs=(whole, whole),
        scratch_shapes=[
            pltpu.VMEM((peers, rows, width), bf16),
            pltpu.VMEM((peers, rows, 2 * units), bf16),
            pltpu.VMEM((planes, rows, units), bf16),
            pltpu.VMEM((planes, rows, units), bf16),
            pltpu.VMEM((peers, 8, rows), f32),
            pltpu.VMEM((peers, rows, 8), f32),
            pltpu.VMEM((units, width), bf16),
            pltpu.VMEM((rows, units), bf16),
            pltpu.VMEM((rows, units), f32),
            pltpu.VMEM((peers, rows, units), bf16),
            pltpu.VMEM((peers, rows, units), bf16),
            pltpu.VMEM((units, width), f32),
            pltpu.VMEM((half, width), bf16),
            pltpu.VMEM((half, width), bf16),
            dma((planes, 2, CHUNKS)),
            dma((planes, CHUNKS)),
            dma((planes, 2, CHUNKS)),
            dma((planes, CHUNKS)),
            dma((planes, CHUNKS)),
            dma((planes, CHUNKS)),
            dma((planes, CHUNKS)),
            dma((planes, CHUNKS)),
            dma((peers,)),
            dma((peers,)),
            dma((peers,)),
            dma((peers,)),
            dma((2,)),
            dma((2,)),
            dma((2,)),
        ],
        compiler_params=pltpu.CompilerParams(
            collective_id=0, has_side_effects=True, vmem_limit_bytes=48 * 1024 * 1024
        ),
    )(grad_out, pre_act.reshape(rows, 4 * units), routes.T, gate_prob.T, down_weight[0])
    return (d_pre.reshape(rows, 2, 2, units), grad_down[None])


def shards(grad_out, pre_act, routes, gate_prob, down_weight):
    peers, cores = lax.axis_size("expert"), lax.axis_size("dp")
    capacity = 4 * routes.shape[0] * routes.shape[1] // peers
    dense = capacity >= routes.shape[0] and peers % 2 == 0 and cores == 2
    plan = dense_shards if dense else packed_shards
    return plan(grad_out, pre_act, routes, gate_prob, down_weight)


def solution(mesh):
    placed = (
        P(("groups", "expert", "dp"), None),
        P(("groups", "expert", "dp"), None, None, None),
        P(("groups", "expert", "dp"), None),
        P(("groups", "expert", "dp"), None),
        P("expert", "dp", None),
    )
    return jax.shard_map(
        shards,
        mesh=mesh,
        in_specs=placed,
        out_specs=(
            P(("groups", "expert", "dp"), None, None, None),
            P(("groups", "expert"), "dp", None),
        ),
        check_vma=False,
    )
```

```python
import functools

import jax
import jax.numpy as jnp
from jax import lax
from jax.experimental import pallas as pl
from jax.experimental.pallas import tpu as pltpu
from jax.sharding import PartitionSpec as P


def gate_hidden(gate_pre, up_pre):
    sigmoid_gate = jax.nn.sigmoid(gate_pre)
    return (gate_pre * sigmoid_gate * up_pre).astype(jnp.bfloat16)


def activation_grads(hidden_grad, gate_pre, up_pre):
    sigmoid_gate = jax.nn.sigmoid(gate_pre)
    upstream = hidden_grad.astype(jnp.float32)
    gate_part = upstream * up_pre * sigmoid_gate * (1.0 + gate_pre * (1.0 - sigmoid_gate))
    up_part = upstream * (gate_pre * sigmoid_gate)
    return jnp.concatenate([gate_part, up_part], axis=-1).astype(jnp.bfloat16)


def pack_rows(row_values, slot_index, peer_count, capacity):
    row_width = row_values.shape[1]
    buffer = (
        jnp.zeros((peer_count * capacity, row_width), row_values.dtype)
        .at[slot_index]
        .set(row_values)
    )
    return buffer.reshape(peer_count, capacity, row_width)


def expert_work(scaled_rows, hidden_rows, full_weight):
    dims_back = (((1,), (1,)), ((), ()))
    dims_outer = (((0,), (0,)), ((), ()))
    hidden_grad = lax.dot_general(
        scaled_rows, full_weight, dims_back, preferred_element_type=jnp.float32
    ).astype(jnp.bfloat16)
    partial_value = lax.dot_general(
        hidden_rows, scaled_rows, dims_outer, preferred_element_type=jnp.float32
    )
    return (hidden_grad, partial_value)


def balanced_work(got_scaled, got_hidden, full_weight):
    peer_count = got_scaled.shape[0]
    capacity = got_scaled.shape[1]
    slots_all = peer_count * capacity
    scaled_rows = got_scaled.reshape(slots_all, got_scaled.shape[2])
    hidden_rows = got_hidden.reshape(slots_all, got_hidden.shape[2])
    hidden_grad, partial_value = expert_work(scaled_rows, hidden_rows, full_weight)
    return (hidden_grad.reshape(peer_count, capacity, hidden_grad.shape[1]), partial_value)


def packed_shards(grad_out, pre_act, routes, gate_prob, down_weight):
    peer_count = lax.axis_size("expert")
    token_rows = routes.shape[0]
    route_width = routes.shape[1]
    route_count = token_rows * route_width
    capacity = 4 * route_count // peer_count
    feature_count = grad_out.shape[1]
    hidden_count = pre_act.shape[3]
    scaled = (
        (gate_prob[:, :, None] * grad_out[:, None, :].astype(jnp.float32))
        .astype(jnp.bfloat16)
        .reshape(route_count, feature_count)
    )
    pre_rows = pre_act.reshape(route_count, 2 * hidden_count)
    expert_ids = routes.reshape(route_count)
    one_hot = (expert_ids[:, None] == jnp.arange(peer_count, dtype=jnp.int32)[None, :]).astype(
        jnp.int32
    )
    slot_rank = jnp.sum(jnp.cumsum(one_hot, axis=0) * one_hot, axis=1) - 1
    sent_counts = jnp.sum(one_hot, axis=0).reshape(peer_count, 1)
    slot_index = expert_ids * capacity + slot_rank
    full_weight = lax.all_gather(down_weight[0], "dp", axis=0, tiled=True)
    got_scaled, got_pre, arrived = (
        lax.all_to_all(
            pack_rows(scaled, slot_index, peer_count, capacity),
            "expert",
            split_axis=0,
            concat_axis=0,
            tiled=True,
        ),
        lax.all_to_all(
            pack_rows(pre_rows, slot_index, peer_count, capacity),
            "expert",
            split_axis=0,
            concat_axis=0,
            tiled=True,
        ),
        lax.all_to_all(sent_counts, "expert", split_axis=0, concat_axis=0, tiled=True),
    )
    pre_float = got_pre.astype(jnp.float32)
    gate_pre = pre_float[:, :, :hidden_count]
    up_pre = pre_float[:, :, hidden_count:]
    got_hidden = gate_hidden(gate_pre, up_pre)
    hidden_grad, partial_value = balanced_work(got_scaled, got_hidden, full_weight)
    slot_grads = activation_grads(hidden_grad, gate_pre, up_pre)
    returned = lax.all_to_all(slot_grads, "expert", split_axis=0, concat_axis=0, tiled=True)
    d_pre = returned.reshape(peer_count * capacity, 2 * hidden_count)[slot_index]
    summed = lax.psum_scatter(
        partial_value.astype(jnp.bfloat16), "dp", scatter_dimension=0, tiled=True
    )
    return (d_pre.reshape(token_rows, route_width, 2, hidden_count), summed[None])


CHUNKS = 4
TILE = 1024
MESH = pl.DeviceIdType.MESH


def source_at(z, turn, planes):
    reach = jnp.minimum(z, planes - 1 - z)
    step = (turn + 1) // 2
    lower = 2 * z <= planes - 1
    odd = jnp.where(turn % 2 == 1, 1, -1)
    near = jnp.where(lower, z + odd * step, z - odd * step)
    far = jnp.where(lower, turn, planes - 1 - turn)
    return jnp.where(turn <= 2 * reach, near, far)


def dense_kernel(
    peers,
    grad_ref,
    pre_ref,
    routes_ref,
    prob_ref,
    weight_ref,
    d_pre_ref,
    down_ref,
    tokens,
    hiddens,
    cross_out,
    cross_in,
    metas,
    columns,
    weight,
    chosen,
    back_sum,
    back_out,
    back_in,
    total,
    half_out,
    half_in,
    zg_send,
    zg_recv,
    zh_send,
    zh_recv,
    xg_send,
    xg_recv,
    xh_send,
    xh_recv,
    back_send,
    back_recv,
    meta_send,
    meta_recv,
    dp_send,
    dp_recv,
    load_sem,
):
    planes = peers // 2
    me = lax.axis_index("expert")
    core = lax.axis_index("dp")
    z, x = me // 2, me % 2
    across = z * 2 + 1 - x
    rows, width = grad_ref.shape
    units = weight.shape[0]
    half = units // 2
    part = rows // CHUNKS
    low = pl.multiple_of(core * half, half)
    other = pl.multiple_of((1 - core) * half, half)

    def remote(src, dst, send, recv, where):
        return pltpu.make_async_remote_copy(
            src_ref=src,
            dst_ref=dst,
            send_sem=send,
            recv_sem=recv,
            device_id=where,
            device_id_type=MESH,
        )

    def z_copies(source, way, k):
        slot = source * 2 + x
        span = pl.ds(k * part, part)
        to = {"expert": me + 2 if way == 0 else me - 2}
        return (
            remote(
                tokens.at[slot, span], tokens.at[slot, span],
                zg_send.at[source, way, k], zg_recv.at[source, k], to,
            ),
            remote(
                hiddens.at[slot, span], hiddens.at[slot, span],
                zh_send.at[source, way, k], zh_recv.at[source, k], to,
            ),
        )

    def x_tokens(source, k, column):
        slot = source * 2 + column
        span = pl.ds(k * part, part)
        return remote(
            tokens.at[slot, span], tokens.at[slot, span],
            xg_send.at[source, k], xg_recv.at[source, k], {"expert": across},
        )

    def x_hidden(source, k):
        span = pl.ds(k * part, part)
        return remote(
            cross_out.at[source, span], cross_in.at[source, span],
            xh_send.at[source, k], xh_recv.at[source, k], {"expert": across},
        )

    def back_copy(slot):
        return remote(
            back_out.at[slot], back_in.at[me], back_send.at[slot], back_recv.at[me], {"expert": slot}
        )

    def meta_copy(slot):
        return remote(
            metas.at[me], metas.at[me], meta_send.at[slot], meta_recv.at[me], {"expert": slot}
        )

    def weight_copy():
        return remote(
            weight.at[pl.ds(low, half)], weight.at[pl.ds(low, half)], dp_send.at[0], dp_recv.at[0], {"dp": 1 - core}
        )

    def half_copy():
        return remote(half_out, half_in, dp_send.at[1], dp_recv.at[1], {"dp": 1 - core})

    def moves_up(source):
        return jnp.logical_and(source <= z, z < planes - 1)

    def moves_down(source):
        return jnp.logical_and(source >= z, z > 0)

    def each_peer(body):
        def step(slot, carry):
            @pl.when(slot != me)
            def _():
                body(slot)

            return carry

        lax.fori_loop(0, peers, step, 0)

    barrier = pltpu.get_barrier_semaphore()
    each_peer(
        lambda slot: pl.semaphore_signal(
            barrier, inc=1, device_id={"expert": slot}, device_id_type=MESH
        )
    )
    pl.semaphore_signal(barrier, inc=1, device_id={"dp": 1 - core}, device_id_type=MESH)

    metas[me] = jnp.zeros((8, rows), jnp.float32)
    metas[me, 0:2] = routes_ref[...].astype(jnp.float32)
    metas[me, 2:4] = prob_ref[...]
    load_tokens = pltpu.make_async_copy(grad_ref, tokens.at[me], load_sem.at[0])
    load_tokens.start()
    load_weight = pltpu.make_async_copy(
        weight_ref, weight.at[pl.ds(low, half)], load_sem.at[1]
    )
    load_weight.start()
    for route in range(2):
        base = route * 2 * units
        gate = pre_ref[:, base : base + units].astype(jnp.float32)
        up = pre_ref[:, base + units : base + 2 * units].astype(jnp.float32)
        hiddens[me, :, route * units : (route + 1) * units] = gate_hidden(gate, up)

    pl.semaphore_wait(barrier, peers)
    load_tokens.wait()
    each_peer(lambda slot: meta_copy(slot).start())

    def pick(slot, k, expert):
        span = pl.ds(k * part, part)
        table = columns[slot, span]
        wanted = expert.astype(jnp.float32)
        first = hiddens[slot, span, :units].astype(jnp.float32)
        second = hiddens[slot, span, units:].astype(jnp.float32)
        rest = jnp.where(table[:, 1:2] == wanted, second, 0.0)
        return jnp.where(table[:, 0:1] == wanted, first, rest).astype(jnp.bfloat16)

    def forward_z(source, k):
        @pl.when(moves_up(source))
        def _():
            for copy in z_copies(source, 0, k):
                copy.start()

        @pl.when(moves_down(source))
        def _():
            for copy in z_copies(source, 1, k):
                copy.start()

    for k in range(CHUNKS):
        forward_z(z, k)
        x_tokens(z, k, x).start()
    load_weight.wait()
    weight_copy().start()
    total[...] = jnp.zeros_like(total)
    columns[me] = jnp.transpose(metas[me])

    def take_meta(slot):
        remote(
            metas.at[slot], metas.at[slot], meta_send.at[slot], meta_recv.at[slot], {"expert": slot}
        ).wait_recv()
        columns[slot] = jnp.transpose(metas[slot])

    each_peer(take_meta)
    remote(
        weight.at[pl.ds(other, half)], weight.at[pl.ds(other, half)], dp_send.at[0], dp_recv.at[0], {"dp": 1 - core}
    ).wait_recv()

    def work(slot, now):
        table = columns[slot]
        wanted = me.astype(jnp.float32)
        factor = jnp.where(
            table[:, 0:1] == wanted,
            table[:, 2:3],
            jnp.where(table[:, 1:2] == wanted, table[:, 3:4], 0.0),
        )
        back_sum[...] = jnp.zeros_like(back_sum)

        def tile(j, carry):
            span = pl.ds(pl.multiple_of(j * TILE, TILE), TILE)
            scaled = (factor * tokens[slot, :, span].astype(jnp.float32)).astype(jnp.bfloat16)
            total[:, span] += lax.dot_general(
                chosen[...], scaled, (((0,), (0,)), ((), ())), preferred_element_type=jnp.float32
            )
            back_sum[...] += lax.dot_general(
                scaled, weight[:, span], (((1,), (1,)), ((), ())), preferred_element_type=jnp.float32
            )
            return carry

        lax.fori_loop(0, width // TILE, tile, 0)

        @pl.when(slot == me)
        def _():
            back_in[me] = back_sum[...].astype(jnp.bfloat16)

        @pl.when(slot != me)
        def _():
            back_out[slot] = back_sum[...].astype(jnp.bfloat16)

            @pl.when(now)
            def _():
                back_copy(slot).start()

    edge = jnp.logical_or(z == 0, z == planes - 1)

    def now_at(turn):
        return jnp.logical_or(edge, turn >= planes - 1)

    def turn_step(turn, carry):
        @pl.when(turn < planes)
        def _():
            source = source_at(z, turn, planes)
            slot = source * 2 + x
            for k in range(CHUNKS):
                @pl.when(turn > 0)
                def _():
                    for copy in z_copies(source, 0, k):
                        copy.wait_recv()
                    forward_z(source, k)
                    x_tokens(source, k, x).start()

                span = pl.ds(k * part, part)
                cross_out[source, span] = pick(slot, k, across)
                x_hidden(source, k).start()

        @pl.when(jnp.logical_and(turn == planes - 1, jnp.logical_not(edge)))
        def _():
            def release(index, carry):
                slot = source_at(z, index // 2, planes) * 2 + (x + index % 2) % 2

                @pl.when(slot != me)
                def _():
                    back_copy(slot).start()

                return carry

            lax.fori_loop(0, 2 * planes - 3, release, 0)

        def side(column, inner):
            @pl.when(jnp.logical_and(column == 0, turn < planes))
            def _():
                slot = source_at(z, turn, planes) * 2 + x
                for k in range(CHUNKS):
                    chosen[pl.ds(k * part, part)] = pick(slot, k, me)

            @pl.when(jnp.logical_and(column == 1, turn > 0))
            def _():
                source = source_at(z, turn - 1, planes)
                for k in range(CHUNKS):
                    x_tokens(source, k, 1 - x).wait_recv()
                    x_hidden(source, k).wait_recv()
                chosen[...] = cross_in[source]

            @pl.when(jnp.where(column == 0, turn < planes, turn > 0))
            def _():
                source = source_at(z, turn - column, planes)
                work(source * 2 + (x + column) % 2, now_at(turn))

            return inner

        return lax.fori_loop(0, 2, side, carry)

    lax.fori_loop(0, planes + 1, turn_step, 0)

    half_out[...] = total[pl.ds(other, half)].astype(jnp.bfloat16)
    half_copy().start()

    each_peer(
        lambda slot: remote(
            back_out.at[slot], back_in.at[slot], back_send.at[slot], back_recv.at[slot],
            {"expert": slot},
        ).wait_recv()
    )
    mine = columns[me]
    for route in range(2):
        def gather(slot, carry):
            hit = mine[:, route : route + 1] == slot.astype(jnp.float32)
            back_sum[...] = jnp.where(hit, back_in[slot].astype(jnp.float32), back_sum[...])
            return carry

        lax.fori_loop(0, peers, gather, 0)
        base = route * 2 * units
        gate = pre_ref[:, base : base + units].astype(jnp.float32)
        up = pre_ref[:, base + units : base + 2 * units].astype(jnp.float32)
        d_pre_ref[:, base : base + 2 * units] = activation_grads(back_sum[...], gate, up)

    half_copy().wait_recv()
    kept = total[pl.ds(low, half)].astype(jnp.bfloat16).astype(jnp.float32)
    down_ref[...] = (kept + half_in[...].astype(jnp.float32)).astype(jnp.bfloat16)

    weight_copy().wait_send()
    half_copy().wait_send()

    def drain(slot):
        back_copy(slot).wait_send()
        meta_copy(slot).wait_send()

    each_peer(drain)

    def drain_plane(source, carry):
        for k in range(CHUNKS):
            x_tokens(source, k, x).wait_send()
            x_hidden(source, k).wait_send()

            @pl.when(moves_up(source))
            def _():
                for copy in z_copies(source, 0, k):
                    copy.wait_send()

            @pl.when(moves_down(source))
            def _():
                for copy in z_copies(source, 1, k):
                    copy.wait_send()

        return carry

    lax.fori_loop(0, planes, drain_plane, 0)


def dense_shards(grad_out, pre_act, routes, gate_prob, down_weight):
    peers = lax.axis_size("expert")
    planes = peers // 2
    rows, width = grad_out.shape
    units = pre_act.shape[3]
    half = down_weight.shape[1]
    whole = pl.BlockSpec(memory_space=pltpu.VMEM)
    away = pl.BlockSpec(memory_space=pl.ANY)
    dma = pltpu.SemaphoreType.DMA
    bf16, f32 = jnp.bfloat16, jnp.float32
    d_pre, grad_down = pl.pallas_call(
        functools.partial(dense_kernel, peers),
        out_shape=(
            jax.ShapeDtypeStruct((rows, 4 * units), bf16),
            jax.ShapeDtypeStruct((half, width), bf16),
        ),
        in_specs=[away, whole, whole, whole, away],
        out_specs=(whole, whole),
        scratch_shapes=[
            pltpu.VMEM((peers, rows, width), bf16),
            pltpu.VMEM((peers, rows, 2 * units), bf16),
            pltpu.VMEM((planes, rows, units), bf16),
            pltpu.VMEM((planes, rows, units), bf16),
            pltpu.VMEM((peers, 8, rows), f32),
            pltpu.VMEM((peers, rows, 8), f32),
            pltpu.VMEM((units, width), bf16),
            pltpu.VMEM((rows, units), bf16),
            pltpu.VMEM((rows, units), f32),
            pltpu.VMEM((peers, rows, units), bf16),
            pltpu.VMEM((peers, rows, units), bf16),
            pltpu.VMEM((units, width), f32),
            pltpu.VMEM((half, width), bf16),
            pltpu.VMEM((half, width), bf16),
            dma((planes, 2, CHUNKS)),
            dma((planes, CHUNKS)),
            dma((planes, 2, CHUNKS)),
            dma((planes, CHUNKS)),
            dma((planes, CHUNKS)),
            dma((planes, CHUNKS)),
            dma((planes, CHUNKS)),
            dma((planes, CHUNKS)),
            dma((peers,)),
            dma((peers,)),
            dma((peers,)),
            dma((peers,)),
            dma((2,)),
            dma((2,)),
            dma((2,)),
        ],
        compiler_params=pltpu.CompilerParams(
            collective_id=0, has_side_effects=True, vmem_limit_bytes=48 * 1024 * 1024
        ),
    )(grad_out, pre_act.reshape(rows, 4 * units), routes.T, gate_prob.T, down_weight[0])
    return (d_pre.reshape(rows, 2, 2, units), grad_down[None])


def shards(grad_out, pre_act, routes, gate_prob, down_weight):
    peers, cores = lax.axis_size("expert"), lax.axis_size("dp")
    capacity = 4 * routes.shape[0] * routes.shape[1] // peers
    dense = capacity >= routes.shape[0] and peers % 2 == 0 and cores == 2
    plan = dense_shards if dense else packed_shards
    return plan(grad_out, pre_act, routes, gate_prob, down_weight)


def solution(mesh):
    placed = (
        P(("groups", "expert", "dp"), None),
        P(("groups", "expert", "dp"), None, None, None),
        P(("groups", "expert", "dp"), None),
        P(("groups", "expert", "dp"), None),
        P("expert", "dp", None),
    )
    return jax.shard_map(
        shards,
        mesh=mesh,
        in_specs=placed,
        out_specs=(
            P(("groups", "expert", "dp"), None, None, None),
            P(("groups", "expert"), "dp", None),
        ),
        check_vma=False,
    )
```
